256 devices in a mesh: leaf: 16 (over z, core), row: 4 (over y), col: 4 (over x).
Axes of the slice: x: 4, y: 4, z: 8, core: 2. Of those that a mesh axis runs over, the one named last changes fastest.
Arguments:
- sketch_leaf: bfloat16 [131072, 256], P(('leaf', 'row'), 'col'), may hold values from -6 to 6
- sketch_sep: bfloat16 [8192, 256], P(('row', 'col')), may hold values from -6 to 6
- leaf_inverse: bfloat16 [131072, 8192], P(('leaf', 'col'), 'row'), as said below
- coupling: bfloat16 [131072, 2048], P(('leaf', 'col'), 'row'), may hold values from -0.0625 to 0.0625
- sep_inverse: bfloat16 [8192, 8192], P('leaf', ('row', 'col'))
- front_map: int32 [16, 16], replicated, may hold values from 0 to 63, as said below
Outputs:
- sketch_out_leaf: float32 [131072, 256], P(('leaf', 'row'), 'col')
- sketch_out_sep: float32 [8192, 256], P(('row', 'col'))
The draws below stay inside these ranges and needn't reach their ends.
Inputs may be any that keep to these rules, and one draw needn't show every extreme that they name: `front_map`: row block q of every section's coupling lies in separator blocks q * 4 to q * 4 + 3. leaf_inverse and sep_inverse are inverses of lower triangular factor blocks (in natural order), stored in block-cyclic order.
All inputs are finite; a program needn't handle non-finite values.
Results may differ from the reference program's by a relative error of at most 0.024.
Values may be sent and summed in bfloat16 or wider, within the bound.
A program may use at most 64 MiB of HBM per device.

```python
import jax
import jax.numpy as jnp
from jax import lax

LN = 8192
K = 256
BLK = 128
GROUP = 4
NBB = 16
NB = 2048
NSB = 64
NS = 8192
N_LEAF = 16
N_ROW = 4
N_COL = 4


def natural_order(count, parts, block):
    index = jnp.arange(count, dtype=jnp.int32)
    share = count // parts
    owner = index // share
    inside = index % share
    return (inside // block * parts + owner) * block + inside % block


def triangle_inverse(key, count, row_parts, col_parts):
    row_nat = natural_order(count, row_parts, BLK)
    col_nat = natural_order(count, col_parts, BLK)
    key_off, key_diag = jax.random.split(key)
    values = jax.random.normal(key_off, (count, count), jnp.float32) * (0.8 / count ** 0.5)
    diag_vals = 1.0 + 0.5 * jax.random.uniform(key_diag, (count, count), jnp.float32)
    lower = row_nat[:, None] > col_nat[None, :]
    on_diag = row_nat[:, None] == col_nat[None, :]
    return jnp.where(on_diag, diag_vals, jnp.where(lower, values, 0.0))


def draw_leaf_inverse(key, part):
    keys = jax.random.split(jax.random.fold_in(key, 11), N_LEAF)

    def one_section(sub_key):
        return triangle_inverse(sub_key, LN, N_COL, N_ROW).astype(jnp.bfloat16)
    blocks = lax.map(one_section, keys)
    return blocks.reshape(N_LEAF * LN, LN)


def draw_sep_inverse(key, part):
    return triangle_inverse(jax.random.fold_in(key, 23), NS, N_LEAF, N_ROW * N_COL).astype(jnp.bfloat16)


def draw_front_map(key, part):
    slots = jax.random.randint(jax.random.fold_in(key, 37), (N_LEAF, NBB), 0, GROUP, dtype=jnp.int32)
    return jnp.arange(NBB, dtype=jnp.int32)[None, :] * GROUP + slots


def shard_levels(own_key, shape, shards, low, high):
    gain = 1.0
    for axis_at, blocks in shards:
        heights = jax.random.uniform(jax.random.fold_in(jax.random.fold_in(own_key, 6), axis_at), (blocks,), jnp.float32, low / len(shards), high / len(shards))
        gain = gain * jnp.repeat(jnp.exp(heights), shape[axis_at] // blocks).reshape((-1,) + (1,) * (len(shape) - 1 - axis_at))
    return gain


def gaussian(rng, shape, spread, bound, pieces=(), held_as=jnp.bfloat16):
    values = jax.random.normal(rng, shape, jnp.float32) * spread
    if len(pieces) > 0:
        values = shard_levels(rng, shape, pieces, -0.22, 0.18) * values
    return jnp.clip(values, min=-bound, max=bound).astype(held_as)


def setup_inputs(seed: int = 0) -> dict:
    arg_keys = jax.random.split(jax.random.key(seed), 7)
    sketch_leaf = gaussian(arg_keys[0], (N_LEAF * LN, K), 1.0, 6.0, ((0, 64), (1, 4)))
    sketch_sep = gaussian(arg_keys[1], (NS, K), 1.0, 6.0, ((0, 16),))
    leaf_inverse = draw_leaf_inverse(jax.random.fold_in(arg_keys[6], 71), 0)
    coupling = gaussian(arg_keys[3], (N_LEAF * LN, NB), LN ** -0.5, 0.0625, ((0, 64), (1, 4)))
    sep_inverse = draw_sep_inverse(jax.random.fold_in(arg_keys[6], 71), 0)
    front_map = draw_front_map(jax.random.fold_in(arg_keys[6], 71), 0)
    return dict(sketch_leaf=sketch_leaf, sketch_sep=sketch_sep, leaf_inverse=leaf_inverse, coupling=coupling, sep_inverse=sep_inverse, front_map=front_map)


def contract_rows(left, right):
    return lax.dot_general(left, right, (((0,), (0,)), ((), ())), preferred_element_type=jnp.float32)


def reference(sketch_leaf, sketch_sep, leaf_inverse, coupling, sep_inverse, front_map):
    sketch_blocks = sketch_leaf.reshape(N_LEAF, LN, K)
    inverse_blocks = leaf_inverse.reshape(N_LEAF, LN, LN)
    coupling_blocks = coupling.reshape(N_LEAF, LN, NB)

    def forward(items):
        inverse_s, sketch_s, coupling_s = items
        front_z = jnp.dot(inverse_s, sketch_s, preferred_element_type=jnp.float32).astype(jnp.bfloat16)
        coupled = contract_rows(coupling_s, front_z).astype(jnp.bfloat16)
        return front_z, coupled

    front_z, coupled = lax.map(forward, (inverse_blocks, sketch_blocks, coupling_blocks))
    place = (front_map[:, :, None] == jnp.arange(NSB, dtype=jnp.int32)[None, None, :]).astype(jnp.float32)
    coupled_wide = coupled.astype(jnp.float32).reshape(N_LEAF, NBB, BLK, K)
    total = jnp.einsum("sqb,sqik->bik", place, coupled_wide).reshape(NS, K)
    sep_rhs = (sketch_sep.astype(jnp.float32) - total).astype(jnp.bfloat16)
    sep_mid = jnp.dot(sep_inverse, sep_rhs, preferred_element_type=jnp.float32).astype(jnp.bfloat16)
    sketch_out_sep = contract_rows(sep_inverse, sep_mid)
    sep_round = sketch_out_sep.astype(jnp.bfloat16).reshape(NSB, BLK, K)
    pulled = sep_round[front_map.astype(jnp.int32)].reshape(N_LEAF, NB, K)

    def backward(items):
        inverse_s, coupling_s, front_s, pulled_s = items
        update = jnp.dot(coupling_s, pulled_s, preferred_element_type=jnp.float32)
        leaf_rhs = (front_s.astype(jnp.float32) - update).astype(jnp.bfloat16)
        return contract_rows(inverse_s, leaf_rhs)

    sketch_out_leaf = lax.map(backward, (inverse_blocks, coupling_blocks, front_z, pulled))
    return sketch_out_leaf.reshape(N_LEAF * LN, K), sketch_out_sep
```

```python
import functools

import jax
import jax.numpy as jnp
from jax import lax
from jax.experimental import pallas as pl
from jax.experimental.pallas import tpu as pltpu
from jax.sharding import PartitionSpec as P

MESH = pl.DeviceIdType.MESH
BF16 = jnp.bfloat16
F32 = jnp.float32

N_LEAF, N_ROW, N_COL = 16, 4, 4
NZ = 8
LR = 2048
CM = 512
SQ = 512
BLK = 128
NC = 4
KT = 16
KC = 64
NG = 4
GC = NC // NG
GK = KC * GC
GT = GK // 4
TILE = 256

ORDER = (
    "L0", "L1", "L2", "Z0", "L3", "Z1", "Z2", "C0", "Z3", "U0", "C1", "C2", "U1", "V0",
    "C3", "U2", "S0", "U3", "V1", "S1", "V2", "M0", "S2", "V3", "M1", "S3", "T0", "M2",
    "T1", "M3", "O0", "T2", "O1", "T3", "P0", "O2", "P1", "B0", "O3", "B1", "P2", "R0",
    "P3", "B2", "R1", "Q0", "B3", "Y0", "R2", "Q1", "F0", "R3", "Q2", "F1", "Q3", "F2",
    "F3",
)


def nt(left, right):
    return lax.dot_general(left, right, (((1,), (1,)), ((), ())), preferred_element_type=F32)


def nn(left, right):
    return lax.dot_general(left, right, (((1,), (0,)), ((), ())), preferred_element_type=F32)


def kernel(
    xt, sep, lfac, cfac, sfac, fmap_in,
    out_leaf, out_sep,
    lv, cv, sv, sep_in, sept, ot, fmap, xg, zps, zr, zg, cps, cr, lr, prs, pr, mps, mr, mg, ops, orr, og, pg,
    bps, br, rg, fps, fr,
    load_sem, ssem, rsem,
):
    l, r, c = lax.axis_index("leaf"), lax.axis_index("row"), lax.axis_index("col")
    parity = lax.rem(l, 2)
    z = lax.div(l, 2)
    q = r * N_COL + c

    def xpeer(o):
        return (l, r, lax.rem(c + o, N_COL))

    def ypeer(o):
        return (l, lax.rem(r + o, N_ROW), c)

    def zpeer(o):
        return (lax.rem(l + 2 * o, N_LEAF), r, c)

    def leafpeer(o):
        return (lax.rem(l + o, N_LEAF), r, c)

    def planepeer(o):
        return (l, lax.rem(r + o // 4, N_ROW), lax.rem(c + o % 4, N_COL))

    partner = (l + 1 - 2 * parity, r, c)

    load_l = pltpu.make_async_copy(lfac, lv, load_sem.at[0])
    load_c = pltpu.make_async_copy(cfac, cv, load_sem.at[1])
    load_s = pltpu.make_async_copy(sfac, sv, load_sem.at[2])
    own_x = pltpu.make_async_copy(xt, xg.at[:, c], load_sem.at[3])
    load_sep = pltpu.make_async_copy(sep, sep_in, load_sem.at[4])
    load_map = pltpu.make_async_copy(fmap_in, fmap, load_sem.at[5])
    own_x.start()
    load_sep.start()
    load_map.start()
    load_l.start()
    load_c.start()
    load_s.start()

    barrier = pltpu.get_barrier_semaphore()
    for o in range(1, 16):
        pl.semaphore_signal(barrier, inc=1, device_id=leafpeer(o), device_id_type=MESH)
        pl.semaphore_signal(barrier, inc=1, device_id=planepeer(o), device_id_type=MESH)
    pl.semaphore_wait(barrier, 30)

    sent = []

    def send(src, dst, stage, at, device):
        pltpu.make_async_remote_copy(
            src_ref=src, dst_ref=dst, send_sem=ssem.at[stage, at], recv_sem=rsem.at[stage, at],
            device_id=device, device_id_type=MESH,
        ).start()

    def arrived(ref, stage, at):
        pltpu.make_async_copy(ref, ref, rsem.at[stage, at]).wait()
        sent.append((ref, stage, at))

    for k in range(NC):
        for o in (2, 1, 3):
            send(xt.at[k], xg.at[k, c], 0, k, xpeer(o))
    load_sep.wait()
    load_map.wait()
    sept[...] = sep_in[...].astype(F32).T.astype(BF16).reshape(4, NC, KT, SQ)
    own_x.wait()
    load_l.wait()

    def step_l(k):
        arrived(xg.at[k, pl.ds(0, 3)], 0, k)
        for i in range(LR // TILE):
            depth = (i + 1) * TILE
            part = nt(
                xg[k, :, :, :depth].reshape(KC, depth), lv[i * TILE : depth, :depth]
            )
            zps[k, :, :, i * TILE : depth] = part.astype(BF16).reshape(4, KT, TILE)
        for o in (2, 1, 3):
            peer = ypeer(o)
            send(zps.at[k, peer[1]], zr.at[k, o - 1], 1, k, peer)

    def step_z(k):
        arrived(zr.at[k], 1, k)
        total = zps[k, r].astype(F32)
        for o in range(3):
            total = total + zr[k, o].astype(F32)
        zg[k, r] = total.astype(BF16)
        for o in (2, 1, 3):
            send(zg.at[k, r], zg.at[k, r], 2, k, ypeer(o))

    def step_c(k):
        if k == 0:
            load_c.wait()
        arrived(zg.at[k, pl.ds(0, 3)], 2, k)
        part = nn(zg[k].reshape(KC, LR), cv[...]).astype(BF16)
        for b in range(4):
            cps[k, b] = part[:, b * BLK : (b + 1) * BLK]
        for o in (2, 1, 3):
            peer = xpeer(o)
            send(cps.at[k, peer[2]], cr.at[k, o - 1], 3, k, peer)

    def step_u(g):
        for kk in range(GC):
            k = g * GC + kk
            arrived(cr.at[k], 3, k)
            total = cps[k, c].astype(F32)
            for o in range(3):
                total = total + cr[k, o].astype(F32)
            lr[g, z, kk * KC : (kk + 1) * KC, :] = total.astype(BF16)
        for o in (4, 3, 5, 2, 6, 1, 7):
            send(lr.at[g, z], lr.at[g, z], 4, g, zpeer(o))

    def step_v(g):
        arrived(lr.at[g, pl.ds(0, NZ - 1)], 4, g)
        totals = [jnp.zeros((GK, BLK), F32) for _ in range(4)]
        for s in range(NZ):
            slot = fmap[2 * s + parity, q] - 4 * q
            block = lr[g, s].astype(F32)
            for b in range(4):
                totals[b] = totals[b] + block * jnp.where(slot == b, 1.0, 0.0)
        for b in range(4):
            prs[g, b] = totals[b].astype(BF16)
        send(prs.at[g], pr.at[g], 5, g, partner)

    def step_s(g):
        if g == 0:
            load_s.wait()
        arrived(pr.at[g], 5, g)
        rhs = []
        for b in range(4):
            block = sept[:, g, :, b * BLK : (b + 1) * BLK].reshape(GK, BLK).astype(F32)
            rhs.append((block - (prs[g, b].astype(F32) + pr[g, b].astype(F32))).astype(BF16))
        part = nt(jnp.concatenate(rhs, axis=1), sv[...]).astype(BF16)
        for a in range(4):
            for b in range(4):
                mps[g, a * 4 + b] = part[a * GT : (a + 1) * GT, b * BLK : (b + 1) * BLK]
        for o in (10, 6, 14, 9, 11, 2, 8, 5, 7, 13, 15, 1, 3, 4, 12):
            peer = planepeer(o)
            send(mps.at[g, peer[1] * 4 + peer[2]], mr.at[g, o - 1], 6, g, peer)

    def sum_of(own, others):
        total = own.astype(F32)
        for o in range(15):
            total = total + others(o).astype(F32)
        return total.astype(BF16)

    def wide(ref, g):
        return jnp.concatenate(
            [
                jnp.concatenate([ref[g, a * 4 + b] for a in range(4)], axis=0)
                for b in range(4)
            ],
            axis=1,
        )

    def step_m(g):
        arrived(mr.at[g], 6, g)
        mg[g, q] = sum_of(mps[g, q], lambda o: mr[g, o])
        for o in (10, 6, 14, 9, 11, 2, 8, 5, 7, 13, 15, 1, 3, 4, 12):
            send(mg.at[g, q], mg.at[g, q], 7, g, planepeer(o))

    def step_t(g):
        arrived(mg.at[g, pl.ds(0, 15)], 7, g)
        part = nn(wide(mg, g), sv[...]).astype(BF16)
        for a in range(4):
            for b in range(4):
                ops[g, a * 4 + b] = part[a * GT : (a + 1) * GT, b * BLK : (b + 1) * BLK]
        for o in (8, 7, 9, 6, 10, 5, 11, 4, 12, 3, 13, 2, 14, 1, 15):
            peer = leafpeer(o)
            send(ops.at[g, peer[0]], orr.at[g, o - 1], 8, g, peer)

    def step_o(g):
        arrived(orr.at[g], 8, g)
        og[g, l] = sum_of(ops[g, l], lambda o: orr[g, o])
        for o in (8, 7, 9, 6, 10, 5, 11, 4, 12, 3, 13, 2, 14, 1, 15):
            send(og.at[g, l], og.at[g, l], 9, g, leafpeer(o))

    def step_p(g):
        arrived(og.at[g, pl.ds(0, 15)], 9, g)
        full = wide(og, g).astype(F32)
        slot = fmap[l, q] - 4 * q
        pull = jnp.zeros((GK, BLK), F32)
        for b in range(4):
            pull = pull + full[:, b * BLK : (b + 1) * BLK] * jnp.where(slot == b, 1.0, 0.0)
        pg[g, c] = pull.astype(BF16)
        for o in (2, 1, 3):
            send(pg.at[g, c], pg.at[g, c], 10, g, xpeer(o))
        ot[:, g] = full.reshape(4, KT, SQ)

    def step_b(k):
        g, kk = k // GC, k % GC
        if kk == 0:
            arrived(pg.at[g, pl.ds(0, 3)], 10, g)
        rows = slice(kk * KC, (kk + 1) * KC)
        left = jnp.concatenate([pg[g, b, rows] for b in range(4)], axis=1)
        for i in range(LR // TILE):
            tile = slice(i * TILE, (i + 1) * TILE)
            bps[k, :, :, tile] = nt(left, cv[tile, :]).astype(BF16).reshape(4, KT, TILE)
        for o in (2, 1, 3):
            peer = ypeer(o)
            send(bps.at[k, peer[1]], br.at[k, o - 1], 11, k, peer)

    def step_r(k):
        arrived(br.at[k], 11, k)
        total = bps[k, r].astype(F32)
        for o in range(3):
            total = total + br[k, o].astype(F32)
        rg[k, r] = (zg[k, r].astype(F32) - total).astype(BF16)
        for o in (2, 1, 3):
            send(rg.at[k, r], rg.at[k, r], 12, k, ypeer(o))

    def step_q(k):
        arrived(rg.at[k, pl.ds(0, 3)], 12, k)
        for i in range(LR // TILE):
            first, last = i * TILE, (i + 1) * TILE
            part = nn(
                rg[k, :, :, first:].reshape(KC, LR - first), lv[first:, first:last]
            )
            fps[k, :, :, first:last] = part.astype(BF16).reshape(4, KT, TILE)
        for o in (2, 1, 3):
            peer = xpeer(o)
            send(fps.at[k, peer[2]], fr.at[k, o - 1], 13, k, peer)

    def step_f(k):
        arrived(fr.at[k], 13, k)
        total = fps[k, c].astype(F32)
        for o in range(3):
            total = total + fr[k, o].astype(F32)
        out_leaf[k] = total

    def step_y(_):
        out_sep[...] = ot[...].reshape(4 * NC * KT, SQ).T

    steps = dict(
        L=step_l, Z=step_z, C=step_c, U=step_u, V=step_v, S=step_s, M=step_m, T=step_t,
        O=step_o, P=step_p, B=step_b, R=step_r, Q=step_q, F=step_f, Y=step_y,
    )
    for name in ORDER:
        steps[name[0]](int(name[1]))

    for ref, stage, at in sent:
        pltpu.make_async_copy(ref, ref, ssem.at[stage, at]).wait()


def shards(sketch_leaf, sketch_sep, leaf_inverse, coupling, sep_inverse, front_map):
    xt = sketch_leaf.T.reshape(NC, KT, LR)
    vmem = pl.BlockSpec(memory_space=pltpu.VMEM)
    hbm = pl.BlockSpec(memory_space=pltpu.HBM)
    v = pltpu.VMEM
    leaf_wide = (NC, 4, KT, LR)
    leaf_got = (NC, 3, KT, LR)
    sep_full, sep_got = (NG, 16, GT, BLK), (NG, 15, GT, BLK)
    out_leaf, out_sep = pl.pallas_call(
        kernel,
        out_shape=(
            pltpu.VMEM((NC, KT, LR), F32),
            pltpu.VMEM((SQ, 4 * NC * KT), F32),
        ),
        in_specs=[hbm] * 6,
        out_specs=(vmem, vmem),
        scratch_shapes=[
            v((LR, LR), BF16), v((LR, CM), BF16), v((SQ, SQ), BF16),
            v((SQ, 4 * NC * KT), BF16), v((4, NC, KT, SQ), BF16), v((4, NC, KT, SQ), F32),
            pltpu.SMEM((N_LEAF, 16), jnp.int32),
            v(leaf_wide, BF16),
            v(leaf_wide, BF16), v(leaf_got, BF16), v(leaf_wide, BF16),
            v((NC, 4, KC, BLK), BF16), v((NC, 3, KC, BLK), BF16),
            v((NG, NZ, GK, BLK), BF16),
            v((NG, 4, GK, BLK), BF16), v((NG, 4, GK, BLK), BF16),
            v(sep_full, BF16), v(sep_got, BF16), v(sep_full, BF16),
            v(sep_full, BF16), v(sep_got, BF16), v(sep_full, BF16),
            v((NG, 4, GK, BLK), BF16),
            v(leaf_wide, BF16), v(leaf_got, BF16), v(leaf_wide, BF16),
            v(leaf_wide, BF16), v(leaf_got, BF16),
            pltpu.SemaphoreType.DMA((6,)),
            pltpu.SemaphoreType.DMA((14, NC)),
            pltpu.SemaphoreType.DMA((14, NC)),
        ],
        compiler_params=pltpu.CompilerParams(
            collective_id=0, has_side_effects=True, vmem_limit_bytes=58 << 20
        ),
        cost_estimate=pl.CostEstimate(
            flops=6_000_000_000, bytes_accessed=13_000_000, transcendentals=0
        ),
        name="sketch",
    )(xt, sketch_sep, leaf_inverse, coupling, sep_inverse, front_map)
    out_leaf = out_leaf.reshape(NC * KT, LR).T
    return out_leaf, out_sep


def solution(mesh):
    placed = (
        P(("leaf", "row"), "col"),
        P(("row", "col"), None),
        P(("leaf", "col"), "row"),
        P(("leaf", "col"), "row"),
        P("leaf", ("row", "col")),
        P(),
    )
    return jax.shard_map(
        shards,
        mesh=mesh,
        in_specs=placed,
        out_specs=(P(("leaf", "row"), "col"), P(("row", "col"), None)),
        check_vma=False,
    )
```

```python
import functools

import jax
import jax.numpy as jnp
from jax import lax
from jax.experimental import pallas as pl
from jax.experimental.pallas import tpu as pltpu
from jax.sharding import PartitionSpec as P

MESH = pl.DeviceIdType.MESH
BF16 = jnp.bfloat16
F32 = jnp.float32

N_LEAF, N_ROW, N_COL = 16, 4, 4
LR = 2048
CM = 512
SQ = 512
BLK = 128
NC = 4
KT = 16
KC = 64
NG = 4
GC = NC // NG
GK = KC * GC
TILE = 256

ORDER = (
    "L0", "L1", "L2", "Z0", "L3", "Z1", "Z2", "C0", "Z3", "U0", "C1", "C2", "U1", "S0",
    "U2", "C3", "S1", "U3", "M0", "S2", "M1", "S3", "T0", "M2", "T1", "O0", "M3", "O1",
    "T2", "P0", "T3", "O2", "P1", "B0", "O3", "B1", "P2", "R0", "P3", "B2", "Y0", "R1",
    "B3", "Q0", "R2", "Q1", "F0", "R3", "Q2", "F1", "Q3", "F2", "F3",
)


def nt(left, right):
    return lax.dot_general(left, right, (((1,), (1,)), ((), ())), preferred_element_type=F32)


def nn(left, right):
    return lax.dot_general(left, right, (((1,), (0,)), ((), ())), preferred_element_type=F32)


def kernel(
    xt, sep, lfac, cfac, sfac, fmap_in,
    out_leaf, out_sep,
    lv, cv, sw, sep_in, sept, ot, fmap, xg, zps, zr, zg, cps, cr, ccs, lr, mps, mr, mg, oq, og, pg,
    bps, br, rg, fps, fr,
    load_sem, ssem, rsem, psend, precv,
):
    l, r, c = lax.axis_index("leaf"), lax.axis_index("row"), lax.axis_index("col")
    parity = lax.rem(l, 2)
    z = lax.div(l, 2)
    q = r * N_COL + c

    def xpeer(o):
        return (l, r, lax.rem(c + o, N_COL))

    def ypeer(o):
        return (l, lax.rem(r + o, N_ROW), c)

    def leafpeer(o):
        return (lax.rem(l + o, N_LEAF), r, c)

    own_part = lax.rem(z, 2) * 2 + parity
    side = 1 - 2 * lax.rem(z, 2)
    tile_at = lax.div(z, 2)

    def near(o):
        return (lax.rem(l + 2 * o * side + N_LEAF, N_LEAF), r, c)

    def planepeer(o):
        return (l, lax.rem(r + o // 4, N_ROW), lax.rem(c + o % 4, N_COL))

    partner = (l + 1 - 2 * parity, r, c)
    mate = near(1)
    mate_partner = (mate[0] + 1 - 2 * parity, r, c)

    load_l = pltpu.make_async_copy(lfac, lv, load_sem.at[0])
    load_c = pltpu.make_async_copy(cfac, cv, load_sem.at[1])
    load_s = pltpu.make_async_copy(sfac, sw.at[0], load_sem.at[2])
    own_x = pltpu.make_async_copy(xt, xg.at[:, c], load_sem.at[3])
    load_sep = pltpu.make_async_copy(sep, sep_in, load_sem.at[4])
    load_map = pltpu.make_async_copy(fmap_in, fmap, load_sem.at[5])
    own_x.start()
    load_sep.start()
    load_map.start()
    load_l.start()
    load_c.start()
    load_s.start()

    barrier = pltpu.get_barrier_semaphore()
    greeted = [planepeer(o) for o in range(1, 16)] + [leafpeer(o) for o in range(1, 16)]
    for device in greeted:
        pl.semaphore_signal(barrier, inc=1, device_id=device, device_id_type=MESH)
    pl.semaphore_wait(barrier, len(greeted))

    sent = []

    def send(src, dst, stage, at, device):
        pltpu.make_async_remote_copy(
            src_ref=src, dst_ref=dst, send_sem=ssem.at[stage, at], recv_sem=rsem.at[stage, at],
            device_id=device, device_id_type=MESH,
        ).start()

    def arrived(ref, stage, at):
        pltpu.make_async_copy(ref, ref, rsem.at[stage, at]).wait()
        sent.append((ref, stage, at))

    for k in range(NC):
        for o in (2, 1, 3):
            send(xt.at[k], xg.at[k, c], 0, k, xpeer(o))
    panels = []
    for slot, device in ((3, near(-3)), (2, near(2)), (1, near(-1))):
        for a in range(4):
            area = (pl.ds(a * BLK, BLK), pl.ds(0, (a + 1) * BLK))
            panels.append(
                pltpu.make_async_remote_copy(
                    src_ref=sfac.at[area], dst_ref=sw.at[(slot,) + area],
                    send_sem=psend.at[len(panels)], recv_sem=precv.at[len(panels)],
                    device_id=device, device_id_type=MESH,
                )
            )
    waiting = list(panels)

    def start_panels(count):
        for _ in range(count):
            waiting.pop(0).start()

    start_panels(12)
    load_sep.wait()
    load_map.wait()
    sept[...] = sep_in[...].astype(F32).T.astype(BF16).reshape(4, NC, KT, SQ)
    own_x.wait()
    load_l.wait()

    def step_l(k):
        arrived(xg.at[k, pl.ds(0, 3)], 0, k)
        for i in range(LR // TILE):
            depth = (i + 1) * TILE
            part = nt(
                xg[k, :, :, :depth].reshape(KC, depth), lv[i * TILE : depth, :depth]
            )
            zps[k, :, :, i * TILE : depth] = part.astype(BF16).reshape(4, KT, TILE)
        for o in (2, 1, 3):
            peer = ypeer(o)
            send(zps.at[k, peer[1]], zr.at[k, o - 1], 1, k, peer)
        start_panels(0)

    def step_z(k):
        arrived(zr.at[k], 1, k)
        total = zps[k, r].astype(F32)
        for o in range(3):
            total = total + zr[k, o].astype(F32)
        zg[k, r] = total.astype(BF16)
        for o in (2, 1, 3):
            send(zg.at[k, r], zg.at[k, r], 2, k, ypeer(o))
        if k == 0:
            start_panels(0)

    def step_c(k):
        if k == 0:
            load_c.wait()
        arrived(zg.at[k, pl.ds(0, 3)], 2, k)
        part = nn(zg[k].reshape(KC, LR), cv[...]).astype(BF16)
        for b in range(4):
            cps[k, b] = part[:, b * BLK : (b + 1) * BLK]
        for o in (2, 1, 3):
            peer = xpeer(o)
            send(cps.at[k, peer[2]], cr.at[k, o - 1], 3, k, peer)

    def step_u(g):
        arrived(cr.at[g], 3, g)
        total = cps[g, c].astype(F32)
        for o in range(3):
            total = total + cr[g, o].astype(F32)
        ccs[g] = total.astype(BF16).reshape(4, KT, BLK)
        lr[g, l] = ccs[g, tile_at]
        for o in (8, 7, 9, 6, 10, 5, 11, 4, 12, 3, 13, 2, 14, 1, 15):
            peer = leafpeer(o)
            send(ccs.at[g, lax.div(peer[0], 4)], lr.at[g, l], 4, g, peer)

    def step_s(g):
        if g == 0:
            load_s.wait()
            for panel in panels:
                panel.wait_recv()
        arrived(lr.at[g, pl.ds(0, 15)], 4, g)
        own = sept[tile_at, g].astype(F32)
        rhs = [own[:, b * BLK : (b + 1) * BLK] for b in range(4)]
        for s in range(N_LEAF):
            slot = fmap[s, q] - 4 * q
            block = lr[g, s].astype(F32)
            for b in range(4):
                rhs[b] = rhs[b] - block * jnp.where(slot == b, 1.0, 0.0)
        rhs = jnp.concatenate(rhs, axis=1).astype(BF16)
        for d in range(4):
            for a in range(4):
                depth = (a + 1) * BLK
                part = nt(rhs[:, :depth], sw[d, a * BLK : depth, :depth])
                mps[g, d * 4 + a] = part.astype(BF16)
        for o in (10, 6, 14, 9, 11, 2, 8, 5, 7, 13, 15, 1, 3, 4, 12):
            peer = planepeer(o)
            send(mps.at[g, peer[1] * 4 + peer[2]], mr.at[g, o - 1], 6, g, peer)

    def step_m(g):
        arrived(mr.at[g], 6, g)
        total = mps[g, q].astype(F32)
        for o in range(15):
            total = total + mr[g, o].astype(F32)
        mg[g, q] = total.astype(BF16)
        for o in (10, 6, 14, 9, 11, 2, 8, 5, 7, 13, 15, 1, 3, 4, 12):
            send(mg.at[g, q], mg.at[g, q], 7, g, planepeer(o))

    def step_t(g):
        arrived(mg.at[g, pl.ds(0, 15)], 7, g)
        parts = [jnp.zeros((KT, BLK), F32) for _ in range(4)]
        for d in range(4):
            mid = jnp.concatenate([mg[g, d * 4 + b] for b in range(4)], axis=1)
            for b in range(4):
                first, last = b * BLK, (b + 1) * BLK
                parts[b] = parts[b] + nn(mid[:, first:], sw[d, first:, first:last])
        oq[g, own_part] = jnp.concatenate(parts, axis=1).astype(BF16)
        for device in (mate, mate_partner, partner):
            send(oq.at[g, own_part], oq.at[g, own_part], 8, g, device)

    def step_o(g):
        arrived(oq.at[g, pl.ds(0, 3)], 8, g)
        total = oq[g, 0].astype(F32)
        for o in range(1, 4):
            total = total + oq[g, o].astype(F32)
        og[g, tile_at] = total.astype(BF16)
        for o in (3, 2, 1):
            send(og.at[g, tile_at], og.at[g, tile_at], 9, g, near(-o))

    def step_p(g):
        arrived(og.at[g, pl.ds(0, 3)], 9, g)
        full = og[g].reshape(KC, SQ).astype(F32)
        slot = fmap[l, q] - 4 * q
        pull = jnp.zeros((KC, BLK), F32)
        for b in range(4):
            pull = pull + full[:, b * BLK : (b + 1) * BLK] * jnp.where(slot == b, 1.0, 0.0)
        pg[g, c] = pull.astype(BF16)
        for o in (2, 1, 3):
            send(pg.at[g, c], pg.at[g, c], 10, g, xpeer(o))
        ot[:, g] = full.reshape(4, KT, SQ)

    def step_b(k):
        g, kk = k // GC, k % GC
        if kk == 0:
            arrived(pg.at[g, pl.ds(0, 3)], 10, g)
        rows = slice(kk * KC, (kk + 1) * KC)
        left = jnp.concatenate([pg[g, b, rows] for b in range(4)], axis=1)
        for i in range(LR // TILE):
            tile = slice(i * TILE, (i + 1) * TILE)
            bps[k, :, :, tile] = nt(left, cv[tile, :]).astype(BF16).reshape(4, KT, TILE)
        for o in (2, 1, 3):
            peer = ypeer(o)
            send(bps.at[k, peer[1]], br.at[k, o - 1], 11, k, peer)

    def step_r(k):
        arrived(br.at[k], 11, k)
        total = bps[k, r].astype(F32)
        for o in range(3):
            total = total + br[k, o].astype(F32)
        rg[k, r] = (zg[k, r].astype(F32) - total).astype(BF16)
        for o in (2, 1, 3):
            send(rg.at[k, r], rg.at[k, r], 12, k, ypeer(o))

    def step_q(k):
        arrived(rg.at[k, pl.ds(0, 3)], 12, k)
        for i in range(LR // TILE):
            first, last = i * TILE, (i + 1) * TILE
            part = nn(
                rg[k, :, :, first:].reshape(KC, LR - first), lv[first:, first:last]
            )
            fps[k, :, :, first:last] = part.astype(BF16).reshape(4, KT, TILE)
        for o in (2, 1, 3):
            peer = xpeer(o)
            send(fps.at[k, peer[2]], fr.at[k, o - 1], 13, k, peer)

    def step_f(k):
        arrived(fr.at[k], 13, k)
        total = fps[k, c].astype(F32)
        for o in range(3):
            total = total + fr[k, o].astype(F32)
        out_leaf[k] = total

    def step_y(_):
        out_sep[...] = ot[...].reshape(4 * NC * KT, SQ).T

    steps = dict(
        L=step_l, Z=step_z, C=step_c, U=step_u, S=step_s, M=step_m, T=step_t,
        O=step_o, P=step_p, B=step_b, R=step_r, Q=step_q, F=step_f, Y=step_y,
    )
    for name in ORDER:
        steps[name[0]](int(name[1]))

    for ref, stage, at in sent:
        pltpu.make_async_copy(ref, ref, ssem.at[stage, at]).wait()
    for panel in panels:
        panel.wait_send()


def shards(sketch_leaf, sketch_sep, leaf_inverse, coupling, sep_inverse, front_map):
    xt = sketch_leaf.T.reshape(NC, KT, LR)
    vmem = pl.BlockSpec(memory_space=pltpu.VMEM)
    hbm = pl.BlockSpec(memory_space=pltpu.HBM)
    v = pltpu.VMEM
    leaf_wide = (NC, 4, KT, LR)
    leaf_got = (NC, 3, KT, LR)
    sep_full, sep_got = (NG, 16, KT, BLK), (NG, 15, KT, BLK)
    out_leaf, out_sep = pl.pallas_call(
        kernel,
        out_shape=(
            pltpu.VMEM((NC, KT, LR), F32),
            pltpu.VMEM((SQ, 4 * NC * KT), F32),
        ),
        in_specs=[hbm] * 6,
        out_specs=(vmem, vmem),
        scratch_shapes=[
            v((LR, LR), BF16), v((LR, CM), BF16), v((4, SQ, SQ), BF16),
            v((SQ, 4 * NC * KT), BF16), v((4, NC, KT, SQ), BF16), v((4, NC, KT, SQ), F32),
            pltpu.SMEM((N_LEAF, 16), jnp.int32),
            v(leaf_wide, BF16),
            v(leaf_wide, BF16), v(leaf_got, BF16), v(leaf_wide, BF16),
            v((NC, 4, KC, BLK), BF16), v((NC, 3, KC, BLK), BF16),
            v((NG, 4, KT, BLK), BF16), v((NG, N_LEAF, KT, BLK), BF16),
            v(sep_full, BF16), v(sep_got, BF16), v(sep_full, BF16),
            v((NG, 4, KT, SQ), BF16), v((NG, 4, KT, SQ), BF16),
            v((NG, 4, GK, BLK), BF16),
            v(leaf_wide, BF16), v(leaf_got, BF16), v(leaf_wide, BF16),
            v(leaf_wide, BF16), v(leaf_got, BF16),
            pltpu.SemaphoreType.DMA((6,)),
            pltpu.SemaphoreType.DMA((14, NC)),
            pltpu.SemaphoreType.DMA((14, NC)),
            pltpu.SemaphoreType.DMA((12,)),
            pltpu.SemaphoreType.DMA((12,)),
        ],
        compiler_params=pltpu.CompilerParams(
            collective_id=0, has_side_effects=True, vmem_limit_bytes=58 << 20
        ),
        cost_estimate=pl.CostEstimate(
            flops=6_000_000_000, bytes_accessed=13_000_000, transcendentals=0
        ),
        name="sketch",
    )(xt, sketch_sep, leaf_inverse, coupling, sep_inverse, front_map)
    out_leaf = out_leaf.reshape(NC * KT, LR).T
    return out_leaf, out_sep


def solution(mesh):
    placed = (
        P(("leaf", "row"), "col"),
        P(("row", "col"), None),
        P(("leaf", "col"), "row"),
        P(("leaf", "col"), "row"),
        P("leaf", ("row", "col")),
        P(),
    )
    return jax.shard_map(
        shards,
        mesh=mesh,
        in_specs=placed,
        out_specs=(P(("leaf", "row"), "col"), P(("row", "col"), None)),
        check_vma=False,
    )
```

```python
import functools

import jax
import jax.numpy as jnp
from jax import lax
from jax.experimental import pallas as pl
from jax.experimental.pallas import tpu as pltpu
from jax.sharding import PartitionSpec as P

MESH = pl.DeviceIdType.MESH
BF16 = jnp.bfloat16
F32 = jnp.float32

N_LEAF, N_ROW, N_COL = 16, 4, 4
LR = 2048
CM = 512
SQ = 512
BLK = 128
NC = 4
KT = 16
KC = 64
NG = 4
GC = NC // NG
GK = KC * GC
TILE = 256

ORDER = (
    "L0", "L1", "L2", "Z0", "L3", "Z1", "Z2", "C0", "Z3", "U0", "C1", "C2", "U1", "S0",
    "C3", "U2", "S1", "U3", "M0", "S2", "M1", "S3", "T0", "M2", "T1", "O0", "M3", "T2",
    "O1", "P0", "O2", "T3", "P1", "B0", "O3", "P2", "B1", "B2", "R0", "P3", "R1", "Y0",
    "B3", "R2", "Q0", "Q1", "R3", "F0", "Q2", "F1", "Q3", "F2", "F3",
)


def nt(left, right):
    return lax.dot_general(left, right, (((1,), (1,)), ((), ())), preferred_element_type=F32)


def nn(left, right):
    return lax.dot_general(left, right, (((1,), (0,)), ((), ())), preferred_element_type=F32)


def kernel(
    xt, sep, lfac, cfac, sfac, fmap_in,
    out_leaf, out_sep,
    lv, cv, sw, sep_in, sept, ot, fmap, xg, zps, zr, zg, cps, cr, ccs, lr, mps, mr, mg, oq, og, pg,
    bps, br, rg, fps, fr,
    load_sem, ssem, rsem, psend, precv,
):
    l, r, c = lax.axis_index("leaf"), lax.axis_index("row"), lax.axis_index("col")
    parity = lax.rem(l, 2)
    z = lax.div(l, 2)
    q = r * N_COL + c

    def xpeer(o):
        return (l, r, lax.rem(c + o, N_COL))

    def ypeer(o):
        return (l, lax.rem(r + o, N_ROW), c)

    def leafpeer(o):
        return (lax.rem(l + o, N_LEAF), r, c)

    own_part = lax.rem(z, 2) * 2 + parity
    side = 1 - 2 * lax.rem(z, 2)
    tile_at = lax.div(z, 2)

    def near(o):
        return (lax.rem(l + 2 * o * side + N_LEAF, N_LEAF), r, c)

    def planepeer(o):
        return (l, lax.rem(r + o // 4, N_ROW), lax.rem(c + o % 4, N_COL))

    partner = (l + 1 - 2 * parity, r, c)
    mate = near(1)
    mate_partner = (mate[0] + 1 - 2 * parity, r, c)

    load_l = pltpu.make_async_copy(lfac, lv, load_sem.at[0])
    load_c = pltpu.make_async_copy(cfac, cv, load_sem.at[1])
    load_s = pltpu.make_async_copy(sfac, sw.at[0], load_sem.at[2])
    own_x = pltpu.make_async_copy(xt, xg.at[:, c], load_sem.at[3])
    load_sep = pltpu.make_async_copy(sep, sep_in, load_sem.at[4])
    load_map = pltpu.make_async_copy(fmap_in, fmap, load_sem.at[5])
    own_x.start()
    load_sep.start()
    load_map.start()
    load_l.start()
    load_c.start()
    load_s.start()

    barrier = pltpu.get_barrier_semaphore()
    greeted = [planepeer(o) for o in range(1, 16)] + [leafpeer(o) for o in range(1, 16)]
    for device in greeted:
        pl.semaphore_signal(barrier, inc=1, device_id=device, device_id_type=MESH)
    pl.semaphore_wait(barrier, len(greeted))

    sent = []

    def send(src, dst, stage, at, device):
        pltpu.make_async_remote_copy(
            src_ref=src, dst_ref=dst, send_sem=ssem.at[stage, at], recv_sem=rsem.at[stage, at],
            device_id=device, device_id_type=MESH,
        ).start()

    def left(ref, stage, at):
        pltpu.make_async_copy(ref, ref, ssem.at[stage, at]).wait()

    def arrived(ref, stage, at):
        pltpu.make_async_copy(ref, ref, rsem.at[stage, at]).wait()
        sent.append((ref, stage, at))
        if len(sent) > 8:
            left(*sent.pop(0))

    for k in range(NC):
        for o in (2, 1, 3):
            send(xt.at[k], xg.at[k, c], 0, k, xpeer(o))
    panels = []
    for slot, device in ((3, near(-3)), (2, near(2)), (1, near(-1))):
        for a in range(4):
            area = (pl.ds(a * BLK, BLK), pl.ds(0, (a + 1) * BLK))
            panels.append(
                pltpu.make_async_remote_copy(
                    src_ref=sfac.at[area], dst_ref=sw.at[(slot,) + area],
                    send_sem=psend.at[len(panels)], recv_sem=precv.at[len(panels)],
                    device_id=device, device_id_type=MESH,
                )
            )
    waiting = list(panels)

    def start_panels(count):
        for _ in range(count):
            waiting.pop(0).start()

    start_panels(12)
    load_sep.wait()
    load_map.wait()
    sept[...] = sep_in[...].astype(F32).T.astype(BF16).reshape(4, NC, KT, SQ)
    own_x.wait()
    load_l.wait()

    def step_l(k):
        arrived(xg.at[k, pl.ds(0, 3)], 0, k)
        for i in range(LR // TILE):
            depth = (i + 1) * TILE
            part = nt(
                xg[k, :, :, :depth].reshape(KC, depth), lv[i * TILE : depth, :depth]
            )
            zps[k, :, :, i * TILE : depth] = part.astype(BF16).reshape(4, KT, TILE)
        for o in (2, 1, 3):
            peer = ypeer(o)
            send(zps.at[k, peer[1]], zr.at[k, o - 1], 1, k, peer)
        start_panels(0)

    def step_z(k):
        arrived(zr.at[k], 1, k)
        total = zps[k, r].astype(F32)
        for o in range(3):
            total = total + zr[k, o].astype(F32)
        zg[k, r] = total.astype(BF16)
        for o in (2, 1, 3):
            send(zg.at[k, r], zg.at[k, r], 2, k, ypeer(o))
        if k == 0:
            start_panels(0)

    def step_c(k):
        if k == 0:
            load_c.wait()
        arrived(zg.at[k, pl.ds(0, 3)], 2, k)
        part = nn(zg[k].reshape(KC, LR), cv[...]).astype(BF16)
        for b in range(4):
            cps[k, b] = part[:, b * BLK : (b + 1) * BLK]
        for o in (2, 1, 3):
            peer = xpeer(o)
            send(cps.at[k, peer[2]], cr.at[k, o - 1], 3, k, peer)

    def step_u(g):
        arrived(cr.at[g], 3, g)
        total = cps[g, c].astype(F32)
        for o in range(3):
            total = total + cr[g, o].astype(F32)
        ccs[g] = total.astype(BF16).reshape(4, KT, BLK)
        lr[g, l] = ccs[g, tile_at]
        for o in (8, 7, 9, 6, 10, 5, 11, 4, 12, 3, 13, 2, 14, 1, 15):
            peer = leafpeer(o)
            send(ccs.at[g, lax.div(peer[0], 4)], lr.at[g, l], 4, g, peer)

    def step_s(g):
        if g == 0:
            load_s.wait()
            for panel in panels:
                panel.wait_recv()
        arrived(lr.at[g, pl.ds(0, 15)], 4, g)
        own = sept[tile_at, g].astype(F32)
        rhs = [own[:, b * BLK : (b + 1) * BLK] for b in range(4)]
        for s in range(N_LEAF):
            slot = fmap[s, q] - 4 * q
            block = lr[g, s].astype(F32)
            for b in range(4):
                rhs[b] = rhs[b] - block * jnp.where(slot == b, 1.0, 0.0)
        rhs = jnp.concatenate(rhs, axis=1).astype(BF16)
        for d in range(4):
            for a in range(4):
                depth = (a + 1) * BLK
                part = nt(rhs[:, :depth], sw[d, a * BLK : depth, :depth])
                mps[g, d * 4 + a] = part.astype(BF16)
        for o in (10, 6, 14, 9, 11, 2, 8, 5, 7, 13, 15, 1, 3, 4, 12):
            peer = planepeer(o)
            send(mps.at[g, peer[1] * 4 + peer[2]], mr.at[g, o - 1], 6, g, peer)

    def step_m(g):
        arrived(mr.at[g], 6, g)
        total = mps[g, q].astype(F32)
        for o in range(15):
            total = total + mr[g, o].astype(F32)
        mg[g, q] = total.astype(BF16)
        for o in (10, 6, 14, 9, 11, 2, 8, 5, 7, 13, 15, 1, 3, 4, 12):
            send(mg.at[g, q], mg.at[g, q], 7, g, planepeer(o))

    def step_t(g):
        arrived(mg.at[g, pl.ds(0, 15)], 7, g)
        parts = [jnp.zeros((KT, BLK), F32) for _ in range(4)]
        for d in range(4):
            mid = jnp.concatenate([mg[g, d * 4 + b] for b in range(4)], axis=1)
            for b in range(4):
                first, last = b * BLK, (b + 1) * BLK
                parts[b] = parts[b] + nn(mid[:, first:], sw[d, first:, first:last])
        oq[g, own_part] = jnp.concatenate(parts, axis=1).astype(BF16)
        for device in (mate, mate_partner, partner):
            send(oq.at[g, own_part], oq.at[g, own_part], 8, g, device)

    def step_o(g):
        arrived(oq.at[g, pl.ds(0, 3)], 8, g)
        total = oq[g, 0].astype(F32)
        for o in range(1, 4):
            total = total + oq[g, o].astype(F32)
        og[g, tile_at] = total.astype(BF16)
        for o in (3, 2, 1):
            send(og.at[g, tile_at], og.at[g, tile_at], 9, g, near(-o))

    def step_p(g):
        arrived(og.at[g, pl.ds(0, 3)], 9, g)
        full = og[g].reshape(KC, SQ).astype(F32)
        slot = fmap[l, q] - 4 * q
        pull = jnp.zeros((KC, BLK), F32)
        for b in range(4):
            pull = pull + full[:, b * BLK : (b + 1) * BLK] * jnp.where(slot == b, 1.0, 0.0)
        pg[g, c] = pull.astype(BF16)
        for o in (2, 1, 3):
            send(pg.at[g, c], pg.at[g, c], 10, g, xpeer(o))
        ot[:, g] = full.reshape(4, KT, SQ)

    def step_b(k):
        g, kk = k // GC, k % GC
        if kk == 0:
            arrived(pg.at[g, pl.ds(0, 3)], 10, g)
        rows = slice(kk * KC, (kk + 1) * KC)
        left = jnp.concatenate([pg[g, b, rows] for b in range(4)], axis=1)
        for i in range(LR // TILE):
            tile = slice(i * TILE, (i + 1) * TILE)
            bps[k, :, :, tile] = nt(left, cv[tile, :]).astype(BF16).reshape(4, KT, TILE)
        for o in (2, 1, 3):
            peer = ypeer(o)
            send(bps.at[k, peer[1]], br.at[k, o - 1], 11, k, peer)

    def step_r(k):
        arrived(br.at[k], 11, k)
        total = bps[k, r].astype(F32)
        for o in range(3):
            total = total + br[k, o].astype(F32)
        rg[k, r] = (zg[k, r].astype(F32) - total).astype(BF16)
        for o in (2, 1, 3):
            send(rg.at[k, r], rg.at[k, r], 12, k, ypeer(o))

    def step_q(k):
        arrived(rg.at[k, pl.ds(0, 3)], 12, k)
        for i in range(LR // TILE):
            first, last = i * TILE, (i + 1) * TILE
            part = nn(
                rg[k, :, :, first:].reshape(KC, LR - first), lv[first:, first:last]
            )
            fps[k, :, :, first:last] = part.astype(BF16).reshape(4, KT, TILE)
        for o in (2, 1, 3):
            peer = xpeer(o)
            send(fps.at[k, peer[2]], fr.at[k, o - 1], 13, k, peer)

    def step_f(k):
        arrived(fr.at[k], 13, k)
        total = fps[k, c].astype(F32)
        for o in range(3):
            total = total + fr[k, o].astype(F32)
        out_leaf[k] = total

    def step_y(_):
        out_sep[...] = ot[...].reshape(4 * NC * KT, SQ).T
        for panel in panels:
            panel.wait_send()

    steps = dict(
        L=step_l, Z=step_z, C=step_c, U=step_u, S=step_s, M=step_m, T=step_t,
        O=step_o, P=step_p, B=step_b, R=step_r, Q=step_q, F=step_f, Y=step_y,
    )
    for name in ORDER:
        steps[name[0]](int(name[1]))

    for item in sent:
        left(*item)


def shards(sketch_leaf, sketch_sep, leaf_inverse, coupling, sep_inverse, front_map):
    xt = sketch_leaf.T.reshape(NC, KT, LR)
    vmem = pl.BlockSpec(memory_space=pltpu.VMEM)
    hbm = pl.BlockSpec(memory_space=pltpu.HBM)
    v = pltpu.VMEM
    leaf_wide = (NC, 4, KT, LR)
    leaf_got = (NC, 3, KT, LR)
    sep_full, sep_got = (NG, 16, KT, BLK), (NG, 15, KT, BLK)
    out_leaf, out_sep = pl.pallas_call(
        kernel,
        out_shape=(
            pltpu.VMEM((NC, KT, LR), F32),
            pltpu.VMEM((SQ, 4 * NC * KT), F32),
        ),
        in_specs=[hbm] * 6,
        out_specs=(vmem, vmem),
        scratch_shapes=[
            v((LR, LR), BF16), v((LR, CM), BF16), v((4, SQ, SQ), BF16),
            v((SQ, 4 * NC * KT), BF16), v((4, NC, KT, SQ), BF16), v((4, NC, KT, SQ), F32),
            pltpu.SMEM((N_LEAF, 16), jnp.int32),
            v(leaf_wide, BF16),
            v(leaf_wide, BF16), v(leaf_got, BF16), v(leaf_wide, BF16),
            v((NC, 4, KC, BLK), BF16), v((NC, 3, KC, BLK), BF16),
            v((NG, 4, KT, BLK), BF16), v((NG, N_LEAF, KT, BLK), BF16),
            v(sep_full, BF16), v(sep_got, BF16), v(sep_full, BF16),
            v((NG, 4, KT, SQ), BF16), v((NG, 4, KT, SQ), BF16),
            v((NG, 4, GK, BLK), BF16),
            v(leaf_wide, BF16), v(leaf_got, BF16), v(leaf_wide, BF16),
            v(leaf_wide, BF16), v(leaf_got, BF16),
            pltpu.SemaphoreType.DMA((6,)),
            pltpu.SemaphoreType.DMA((14, NC)),
            pltpu.SemaphoreType.DMA((14, NC)),
            pltpu.SemaphoreType.DMA((12,)),
            pltpu.SemaphoreType.DMA((12,)),
        ],
        compiler_params=pltpu.CompilerParams(
            collective_id=0, has_side_effects=True, vmem_limit_bytes=58 << 20
        ),
        cost_estimate=pl.CostEstimate(
            flops=6_000_000_000, bytes_accessed=13_000_000, transcendentals=0
        ),
        name="sketch",
    )(xt, sketch_sep, leaf_inverse, coupling, sep_inverse, front_map)
    out_leaf = out_leaf.reshape(NC * KT, LR).T
    return out_leaf, out_sep


def solution(mesh):
    placed = (
        P(("leaf", "row"), "col"),
        P(("row", "col"), None),
        P(("leaf", "col"), "row"),
        P(("leaf", "col"), "row"),
        P("leaf", ("row", "col")),
        P(),
    )
    return jax.shard_map(
        shards,
        mesh=mesh,
        in_specs=placed,
        out_specs=(P(("leaf", "row"), "col"), P(("row", "col"), None)),
        check_vma=False,
    )
```
